32 devices in a mesh: comp: 4 (over y, core), tp: 8 (over z, x).
Axes of the slice: x: 2, y: 2, z: 4, core: 2. Of those that a mesh axis runs over, the one named last changes fastest.
Arguments:
- queries: bfloat16 [4, 512, 1024], P('comp', None, 'tp'), may hold values from -8 to 8
- answer_keys: bfloat16 [4, 512, 128], P('comp'), may hold values from -6 to 6
- answer_values: bfloat16 [4, 512, 128], P('comp'), may hold values from -6 to 6
- prompt_keys: bfloat16 [768, 128], P('comp'), may hold values from -8 to 8
- prompt_values: bfloat16 [768, 128], P('comp'), may hold values from -6 to 6
- out_grad: bfloat16 [4, 512, 1024], P('comp', None, 'tp'), may hold values from -6 to 6
- block_counts: int32 [4], replicated, may hold values from 1 to 8, 18 in all
Outputs:
- attended: bfloat16 [4, 512, 1024], P('comp', None, 'tp')
- query_grad: bfloat16 [4, 512, 1024], P('comp', None, 'tp')
- keygrad_prompt: bfloat16 [768, 128], P('comp')
- valgrad_prompt: bfloat16 [768, 128], P('comp')
- keygrad_answer: bfloat16 [4, 512, 128], P('comp')
- valgrad_answer: bfloat16 [4, 512, 128], P('comp')
The draws below stay inside these ranges and needn't reach their ends.
Inputs may be any that keep to these rules, and one draw needn't show every extreme that they name: `block_counts`: the counts add up to 18; the largest is 8.
All inputs are finite; a program needn't handle non-finite values.
Results may differ from the reference program's by a relative error of at most 0.012.
Values may be sent and summed in bfloat16 or wider, within the bound.
A program may use at most 64 MiB of HBM per device.

```python
import math
import jax
import jax.numpy as jnp
import numpy as np
from jax import lax

HD = 128
GROUP = 8
BLK = 64
NBLK = 8
HEADS = 8
KVH = 1
COMP = 4
MAXLEN = 512
LIVE_BLOCKS = 18
PROMPT = 768


def draw_queries(key, part):
    key = jax.random.fold_in(key, 5)
    key_normal, key_spread = jax.random.split(key, 2)
    values = jax.random.normal(key_normal, (COMP, MAXLEN, HEADS, HD), jnp.float32)
    spread = jnp.exp(jax.random.uniform(key_spread, (COMP, MAXLEN, HEADS, 1), jnp.float32, math.log(0.3), math.log(3.0)))
    values = jnp.clip(values * spread, -8.0, 8.0)
    return values.reshape(COMP, MAXLEN, HEADS * HD).astype(jnp.bfloat16)


def draw_prompt_keys(key, part):
    key = jax.random.fold_in(key, 9)
    key_normal, key_spread = jax.random.split(key, 2)
    values = jax.random.normal(key_normal, (PROMPT, KVH, HD), jnp.float32)
    spread = jnp.exp(jax.random.uniform(key_spread, (PROMPT, 1, 1), jnp.float32, math.log(0.5), math.log(1.6)))
    values = jnp.clip(values * spread, -8.0, 8.0)
    return values.reshape(PROMPT, KVH * HD).astype(jnp.bfloat16)


def shard_levels(key, dims, shards, low, largest):
    gain = 1.0
    for dim, blocks in shards:
        steps = jax.random.uniform(jax.random.fold_in(jax.random.fold_in(key, 6), dim), (blocks,), jnp.float32, low / len(shards), largest / len(shards))
        gain = gain * jnp.repeat(jnp.exp(steps), dims[dim] // blocks).reshape((-1,) + (1,) * (len(dims) - 1 - dim))
    return gain


def profile(amount, total, bound, lean):
    loads = [(1 << 20) // math.isqrt(standing ** lean) + 1 for standing in range(2, amount + 1)]
    surplus, counts = total - bound - (amount - 1), [1] * (amount - 1)
    while surplus > 0:
        candidates = [i for i in range(amount - 1) if counts[i] < bound]
        pool, remaining = sum([loads[i] for i in candidates]), surplus
        for i in candidates:
            more = min(bound - counts[i], max(1, remaining * loads[i] // pool), surplus)
            counts[i] = counts[i] + more
            surplus = surplus - more
    return np.array([bound] + counts)


def ragged(rng, number_of, total, limit, slope):
    if number_of == 2:
        one = jax.random.randint(rng, (), max(1, total - limit), min(limit, total - 1) + 1)
        return jnp.stack([one, total - one])
    lengths = jnp.asarray(profile(number_of, total, limit, slope), jnp.int32)
    twos = (number_of - 1) // 2
    giver, receiver = lengths[1:1 + 2 * twos:2], lengths[2:2 + 2 * twos:2]
    slack = jnp.minimum(giver - 1, limit - receiver)
    shifted = jax.random.randint(jax.random.fold_in(rng, 1), (twos,), 0, 1 << 20) % (slack + 1)
    lengths = lengths.at[1:1 + 2 * twos:2].set(giver - shifted).at[2:2 + 2 * twos:2].set(receiver + shifted)
    return lengths[jax.random.permutation(jax.random.fold_in(rng, 2), number_of)]


def noise(rng, shape, deviation, bound, pieces=(), held_as=jnp.bfloat16):
    result = deviation * jax.random.normal(rng, shape, jnp.float32)
    if pieces:
        result = result * shard_levels(rng, shape, pieces, -0.22, 0.18)
    return jnp.clip(result, -bound, bound).astype(held_as)


def setup_inputs(seed: int = 0) -> dict:
    arg_keys = jax.random.split(jax.random.key(seed), 8)
    queries = draw_queries(jax.random.fold_in(arg_keys[7], 71), 0)
    answer_keys = noise(arg_keys[1], (COMP, MAXLEN, KVH * HD), 1.0, 6.0, ((0, 4),))
    answer_values = noise(arg_keys[2], (COMP, MAXLEN, KVH * HD), 1.0, 6.0, ((0, 4),))
    prompt_keys = draw_prompt_keys(jax.random.fold_in(arg_keys[7], 71), 0)
    prompt_values = noise(arg_keys[4], (PROMPT, KVH * HD), 1.0, 6.0, ((0, 4),))
    out_grad = noise(arg_keys[5], (COMP, MAXLEN, HEADS * HD), 1.0, 6.0, ((0, 4), (2, 8)))
    block_counts = ragged(arg_keys[6], COMP, LIVE_BLOCKS, NBLK, 2).astype(jnp.int32)
    return {"queries": queries, "answer_keys": answer_keys, "answer_values": answer_values, "prompt_keys": prompt_keys, "prompt_values": prompt_values, "out_grad": out_grad, "block_counts": block_counts}


NEG = -1.0e30


def reference(queries, answer_keys, answer_values, prompt_keys, prompt_values, out_grad, block_counts):
    factor = HD ** -0.5
    positions = jnp.arange(MAXLEN)
    active = positions[None, :] < (block_counts * BLK)[:, None]
    causal = positions[None, :] <= positions[:, None]

    def barrier_round(value):
        return lax.optimization_barrier(value.astype(jnp.bfloat16)).astype(jnp.float32)

    def one_head(head_index):
        kv_group = head_index // GROUP
        query_f = lax.dynamic_slice_in_dim(queries, head_index * HD, HD, 2).astype(jnp.float32)
        dout_part = lax.dynamic_slice_in_dim(out_grad, head_index * HD, HD, 2) * active[:, :, None].astype(jnp.bfloat16)
        dout_f = dout_part.astype(jnp.float32)
        key_prompt = lax.dynamic_slice_in_dim(prompt_keys, kv_group * HD, HD, 1).astype(jnp.float32)
        value_prompt = lax.dynamic_slice_in_dim(prompt_values, kv_group * HD, HD, 1).astype(jnp.float32)
        key_answer = lax.dynamic_slice_in_dim(answer_keys, kv_group * HD, HD, 2).astype(jnp.float32)
        value_answer = lax.dynamic_slice_in_dim(answer_values, kv_group * HD, HD, 2).astype(jnp.float32)
        score_prompt = jnp.einsum('cld,pd->clp', query_f, key_prompt) * factor
        score_answer = jnp.where(causal[None], jnp.einsum('cld,cmd->clm', query_f, key_answer) * factor, NEG)
        peak = jnp.maximum(score_prompt.max(-1), score_answer.max(-1))
        summed = jnp.sum(jnp.exp(score_prompt - peak[..., None]), -1) + jnp.sum(jnp.exp(score_answer - peak[..., None]), -1)
        log_total = peak + jnp.log(summed)
        prob_prompt = jnp.exp(score_prompt - log_total[..., None])
        prob_answer = jnp.exp(score_answer - log_total[..., None])
        rounded_prompt = barrier_round(prob_prompt)
        rounded_answer = barrier_round(prob_answer)
        mixed = jnp.einsum('clp,pd->cld', rounded_prompt, value_prompt) + jnp.einsum('clm,cmd->cld', rounded_answer, value_answer)
        attended = (mixed * active[:, :, None].astype(jnp.float32)).astype(jnp.bfloat16)
        delta_row = jnp.sum(dout_f * attended.astype(jnp.float32), -1)
        dscore_prompt = prob_prompt * (jnp.einsum('cld,pd->clp', dout_f, value_prompt) - delta_row[..., None])
        dscore_answer = prob_answer * (jnp.einsum('cld,cmd->clm', dout_f, value_answer) - delta_row[..., None])
        scaled_prompt = barrier_round(dscore_prompt * factor)
        scaled_answer = barrier_round(dscore_answer * factor)
        query_grad = (jnp.einsum('clp,pd->cld', scaled_prompt, key_prompt) + jnp.einsum('clm,cmd->cld', scaled_answer, key_answer)).astype(jnp.bfloat16)
        key_term = jnp.einsum('clp,cld->pd', scaled_prompt, query_f)
        value_term = jnp.einsum('clp,cld->pd', rounded_prompt, dout_f)
        answer_key_term = jnp.einsum('clm,cld->cmd', scaled_answer, query_f)
        answer_value_term = jnp.einsum('clm,cld->cmd', rounded_answer, dout_f)
        return attended, query_grad, key_term, value_term, answer_key_term, answer_value_term

    attended, query_grad, key_term, value_term, answer_key_term, answer_value_term = lax.map(one_head, jnp.arange(HEADS))
    attended = jnp.transpose(attended, (1, 2, 0, 3)).reshape(COMP, MAXLEN, HEADS * HD)
    query_grad = jnp.transpose(query_grad, (1, 2, 0, 3)).reshape(COMP, MAXLEN, HEADS * HD)

    def prompt_sum(terms):
        grouped = terms.reshape(KVH, GROUP, PROMPT, HD).sum(1)
        return jnp.transpose(grouped, (1, 0, 2)).reshape(PROMPT, KVH * HD).astype(jnp.bfloat16)

    def answer_sum(terms):
        grouped = terms.reshape(KVH, GROUP, COMP, MAXLEN, HD).sum(1)
        return jnp.transpose(grouped, (1, 2, 0, 3)).reshape(COMP, MAXLEN, KVH * HD).astype(jnp.bfloat16)

    return (attended, query_grad, prompt_sum(key_term), prompt_sum(value_term),
            answer_sum(answer_key_term), answer_sum(answer_value_term))
```

```python
import functools
import jax
import jax.numpy as jnp
from jax import lax
from jax.experimental import pallas as pl
from jax.experimental.pallas import tpu as pltpu
from jax.sharding import PartitionSpec as P

GROUP = 8
BLK = 64
QUAD = 4
COLS = 256
NEG = -1e30
MESH = pl.DeviceIdType.MESH


def contract(left, right, left_dim, right_dim):
    return lax.dot_general(
        left, right, (((left_dim,), (right_dim,)), ((), ())), preferred_element_type=jnp.float32
    )


def kernel(
    n, q_ref, ka_ref, va_ref, kp_ref, vp_ref, do_ref, cnt_ref,
    att_ref, dq_ref, gp_ref, ga_ref,
    k_all, v_all, do_m, st, pb, dsb,
    pown, psend, precv, aown, asend, arecv,
    pxown, pxsend, pxrecv, pzown, pzsend, pzrecv, azown, azsend, azrecv,
    send_sem, recv_sem,
):
    me = lax.axis_index("comp")
    tp = lax.axis_index("tp")
    local = lax.rem(tp, GROUP)
    base = tp - local
    par = lax.rem(local, 2)
    zi = local // 2
    length, hd = q_ref.shape
    shard = kp_ref.shape[0]
    prompt = n * shard
    factor = hd ** (-0.5)
    blocks = length // COLS
    partner = {"tp": base + local + 1 - 2 * par}
    quad = [None] + [{"tp": base + 2 * lax.rem(zi + e, QUAD) + par} for e in range(1, QUAD)]
    comp_to = [None] + [{"comp": lax.rem(me + d, n)} for d in range(1, n)]
    comp_back = [None] + [{"comp": lax.rem(me + n - d, n)} for d in range(1, n)]
    zsrc = [lax.rem(zi + QUAD - e, QUAD) for e in range(QUAD)]

    barrier = pltpu.get_barrier_semaphore()
    peers = comp_to[1:] + [partner] + quad[1:]
    for peer in peers:
        pl.semaphore_signal(barrier, inc=1, device_id=peer, device_id_type=MESH)

    count = [0]
    started = []

    def copy(src, dst, device):
        s = count[0]
        count[0] += 1
        c = pltpu.make_async_remote_copy(
            src_ref=src, dst_ref=dst, send_sem=send_sem.at[s], recv_sem=recv_sem.at[s],
            device_id=device, device_id_type=MESH,
        )
        started.append(c)
        return c

    pl.semaphore_wait(barrier, len(peers))

    k_in, v_in = [], []
    for d in range(1, n):
        k_in.append(copy(kp_ref, k_all.at[pl.ds(d * shard, shard)], comp_to[d]))
        k_in[-1].start()
    for d in range(1, n):
        v_in.append(copy(vp_ref, v_all.at[pl.ds(d * shard, shard)], comp_to[d]))
        v_in[-1].start()

    k_all[:shard] = kp_ref[...]
    k_all[prompt:] = ka_ref[...]
    v_all[:shard] = vp_ref[...]
    v_all[prompt:] = va_ref[...]
    own_count = cnt_ref[me] * BLK
    row = lax.broadcasted_iota(jnp.int32, (length, hd), 0)
    do_m[...] = jnp.where(row < own_count, do_ref[...].astype(jnp.float32), 0.0).astype(jnp.bfloat16)

    def cols(b):
        return slice(b * COLS, (b + 1) * COLS)

    def spans(b):
        return [(d * shard, shard) for d in range(n)] + [(prompt + a * COLS, COLS) for a in range(b + 1)]

    peaks = [None] * blocks

    def scores(b, at, size):
        s = contract(k_all[at:at + size], q_ref[cols(b)], 1, 1) * factor
        if at == prompt + b * COLS:
            m = lax.broadcasted_iota(jnp.int32, s.shape, 0)
            i = lax.broadcasted_iota(jnp.int32, s.shape, 1)
            s = jnp.where(m <= i, s, NEG)
        st[at:at + size, cols(b)] = s
        top = jnp.max(s, axis=0, keepdims=True)
        peaks[b] = top if peaks[b] is None else jnp.maximum(peaks[b], top)

    for b in range(blocks):
        for a in range(b + 1):
            scores(b, prompt + a * COLS, COLS)
        scores(b, 0, shard)
    for d in range(1, n):
        k_in[d - 1].wait_recv()
        for b in range(blocks):
            scores(b, d * shard, shard)

    for b in range(blocks):
        total = jnp.zeros((1, COLS), jnp.float32)
        for at, size in spans(b):
            e = jnp.exp(st[at:at + size, cols(b)] - peaks[b])
            st[at:at + size, cols(b)] = e
            total = total + jnp.sum(e, axis=0, keepdims=True)
        inv = 1.0 / total
        for at, size in spans(b):
            p = st[at:at + size, cols(b)] * inv
            st[at:at + size, cols(b)] = p
            pb[at:at + size, cols(b)] = p.astype(jnp.bfloat16)

    p_in = [[None] * n, [None] * n]

    def prompt_terms(w, probs, right):
        for d in range(n):
            g = jnp.dot(probs[d * shard:(d + 1) * shard], right[...], preferred_element_type=jnp.float32)
            if d == 0:
                pown[w] = g
            else:
                psend[w, d - 1] = g.astype(jnp.bfloat16)
                p_in[w][d] = copy(psend.at[w, d - 1], precv.at[w, d - 1], comp_back[d])
                p_in[w][d].start()

    half = length // 2
    quarter = half // QUAD
    a_in = [None, None]

    def answer_terms(w, probs, right):
        for a in range(blocks):
            at = prompt + a * COLS
            g = jnp.dot(
                probs[at:at + COLS, a * COLS:], right[a * COLS:], preferred_element_type=jnp.float32
            ).reshape(COLS * 2 // length, half, hd)
            first = a * COLS // half
            aown[w, first:first + g.shape[0]] = g
            asend[w, first:first + g.shape[0]] = g.astype(jnp.bfloat16)
        a_in[w] = copy(asend.at[w, 1 - par], arecv.at[w], partner)
        a_in[w].start()

    prompt_terms(1, pb, do_m)
    answer_terms(1, pb, do_m)

    for c in v_in:
        c.wait_recv()
    deltas = []
    for b in range(blocks):
        keys = prompt + (b + 1) * COLS
        mixed = contract(v_all[:keys], pb[:keys, cols(b)], 0, 0)
        lane = lax.broadcasted_iota(jnp.int32, mixed.shape, 1) + b * COLS
        mixed = jnp.where(lane < own_count, mixed, 0.0).astype(jnp.bfloat16).astype(jnp.float32)
        att_ref[cols(b)] = mixed.T.astype(jnp.bfloat16)
        dout_t = do_m[cols(b)].astype(jnp.float32).T
        deltas.append(jnp.sum(dout_t * mixed, axis=0, keepdims=True))

    for b in range(blocks):
        for at, size in spans(b):
            dp = contract(v_all[at:at + size], do_m[cols(b)], 1, 1)
            ds = st[at:at + size, cols(b)] * (dp - deltas[b]) * factor
            dsb[at:at + size, cols(b)] = ds.astype(jnp.bfloat16)

    prompt_terms(0, dsb, q_ref)
    answer_terms(0, dsb, q_ref)

    def quad_scatter(total, own, send, recv):
        size = recv.shape[1]
        own[...] = total.reshape(QUAD, size, hd)
        send[...] = total.astype(jnp.bfloat16).reshape(QUAD, size, hd)
        out = []
        for e in range(1, QUAD):
            c = copy(send.at[lax.rem(zi + e, QUAD)], recv.at[e - 1], quad[e])
            c.start()
            out.append(c)
        return out

    def quad_gather(copies, own, recv, out):
        total = own[zi]
        for e in range(1, QUAD):
            copies[e - 1].wait_recv()
            total = total + recv[e - 1].astype(jnp.float32)
        out[zi] = total.astype(jnp.bfloat16)
        zs = []
        for e in range(1, QUAD):
            c = copy(out.at[zi], out.at[zi], quad[e])
            c.start()
            zs.append(c)
        return zs

    waits = []

    def landed(c, ref):
        pltpu.make_async_remote_copy(
            src_ref=ref, dst_ref=ref, send_sem=c[1], recv_sem=c[2], device_id=partner, device_id_type=MESH
        ).wait_recv()

    def finish_start(mine):
        s = count[0]
        c = copy(mine.at[zi], mine.at[zi], partner)
        c.start()
        return s

    def finish_forward(first, zs, mine):
        for e in range(1, QUAD):
            landed((None, send_sem.at[zs[e - 1]], recv_sem.at[zs[e - 1]]), mine.at[zsrc[e]])
            c = copy(mine.at[zsrc[e]], mine.at[zsrc[e]], partner)
            c.start()

    def answer_scatter(w):
        a_in[w].wait_recv()
        return quad_scatter(
            aown[w, par] + arecv[w].astype(jnp.float32), azown.at[w], azsend.at[w], azrecv.at[w]
        )

    av = answer_scatter(1)
    for b in range(blocks):
        keys = prompt + (b + 1) * COLS
        dq = contract(k_all[:keys], dsb[:keys, cols(b)], 0, 0)
        dq_ref[cols(b)] = dq.T.astype(jnp.bfloat16)

    for w in (1, 0):
        total = pown[w]
        for d in range(1, n):
            p_in[w][d].wait_recv()
            total = total + precv[w, d - 1].astype(jnp.float32)
        pxown[w] = total
        pxsend[w] = total.astype(jnp.bfloat16)
    p_x = copy(pxsend.at[1 - par], pxrecv, partner)
    p_x.start()
    ak = answer_scatter(0)
    p_x.wait_recv()
    ap = quad_scatter(pxown[par] + pxrecv[...].astype(jnp.float32), pzown, pzsend, pzrecv)

    chunks = [
        (av, azown.at[1], azrecv.at[1], ga_ref.at[1, par], ga_ref.at[1, 1 - par]),
        (ak, azown.at[0], azrecv.at[0], ga_ref.at[0, par], ga_ref.at[0, 1 - par]),
        (ap, pzown, pzrecv, gp_ref.at[par], gp_ref.at[1 - par]),
    ]
    state = []
    for copies, own, recv, mine, other in chunks:
        z0 = count[0]
        quad_gather(copies, own, recv, mine)
        x0 = finish_start(mine)
        state.append((z0, x0))
    forwards = []
    for (copies, own, recv, mine, other), (z0, x0) in zip(chunks, state):
        f0 = count[0]
        finish_forward(x0, [z0, z0 + 1, z0 + 2], mine)
        forwards.append(f0)
    for (copies, own, recv, mine, other), (z0, x0), f0 in zip(chunks, state, forwards):
        for e, s in enumerate([x0, f0, f0 + 1, f0 + 2]):
            landed((None, send_sem.at[s], recv_sem.at[s]), other.at[zsrc[e]])
    for c in started:
        c.wait_send()


def fused(queries, answer_keys, answer_values, prompt_keys, prompt_values, out_grad, block_counts, n):
    length, hd = queries.shape
    shard = prompt_keys.shape[0]
    keys = n * shard + length
    half = length // 2
    quarter = half // QUAD
    piece = shard // QUAD
    bf, f32 = jnp.bfloat16, jnp.float32
    sems = 4 * (n - 1) + 2 + 1 + 3 * (3 + 3 + 4)
    vmem = pl.BlockSpec(memory_space=pltpu.VMEM)
    return pl.pallas_call(
        functools.partial(kernel, n),
        out_shape=(
            jax.ShapeDtypeStruct((length, hd), bf),
            jax.ShapeDtypeStruct((length, hd), bf),
            jax.ShapeDtypeStruct((2, QUAD, piece, hd), bf),
            jax.ShapeDtypeStruct((2, 2, QUAD, quarter, hd), bf),
        ),
        in_specs=[vmem] * 6 + [pl.BlockSpec(memory_space=pltpu.SMEM)],
        out_specs=(vmem,) * 4,
        scratch_shapes=[
            pltpu.VMEM((keys, hd), bf),
            pltpu.VMEM((keys, hd), bf),
            pltpu.VMEM((length, hd), bf),
            pltpu.VMEM((keys, length), f32),
            pltpu.VMEM((keys, length), bf),
            pltpu.VMEM((keys, length), bf),
            pltpu.VMEM((2, shard, hd), f32),
            pltpu.VMEM((2, n - 1, shard, hd), bf),
            pltpu.VMEM((2, n - 1, shard, hd), bf),
            pltpu.VMEM((2, 2, half, hd), f32),
            pltpu.VMEM((2, 2, half, hd), bf),
            pltpu.VMEM((2, half, hd), bf),
            pltpu.VMEM((2, shard, hd), f32),
            pltpu.VMEM((2, shard, hd), bf),
            pltpu.VMEM((shard, hd), bf),
            pltpu.VMEM((QUAD, piece, hd), f32),
            pltpu.VMEM((QUAD, piece, hd), bf),
            pltpu.VMEM((QUAD - 1, piece, hd), bf),
            pltpu.VMEM((2, QUAD, quarter, hd), f32),
            pltpu.VMEM((2, QUAD, quarter, hd), bf),
            pltpu.VMEM((2, QUAD - 1, quarter, hd), bf),
            pltpu.SemaphoreType.DMA((sems,)),
            pltpu.SemaphoreType.DMA((sems,)),
        ],
        compiler_params=pltpu.CompilerParams(
            collective_id=0, has_side_effects=True, vmem_limit_bytes=48 * 1024 * 1024
        ),
    )(queries, answer_keys, answer_values, prompt_keys, prompt_values, out_grad, block_counts)


def shards(n, groups, queries, answer_keys, answer_values, prompt_keys, prompt_values, out_grad, block_counts):
    hd = queries.shape[2]
    length = queries.shape[1]
    shard = prompt_keys.shape[0]
    kv = [answer_keys[0], answer_values[0], prompt_keys, prompt_values]
    if groups > 1:
        kv_group = lax.axis_index("tp") // GROUP
        kv = [lax.dynamic_slice_in_dim(x, kv_group * hd, hd, 1) for x in kv]
    attended, query_grad, gp, ga = fused(queries[0], *kv, out_grad[0], block_counts, n)
    outs = [gp[0].reshape(shard, hd), gp[1].reshape(shard, hd), ga[0].reshape(length, hd), ga[1].reshape(length, hd)]
    if groups > 1:
        sets = [[g * GROUP + i for g in range(groups)] for i in range(GROUP)]
        outs = [lax.all_gather(x, "tp", axis=1, tiled=True, axis_index_groups=sets) for x in outs]
    return attended[None], query_grad[None], outs[0], outs[1], outs[2][None], outs[3][None]


def solution(mesh):
    n, tp = mesh.shape["comp"], mesh.shape["tp"]
    return jax.shard_map(
        functools.partial(shards, n, tp // GROUP),
        mesh=mesh,
        in_specs=(
            P("comp", None, "tp"),
            P("comp", None, None),
            P("comp", None, None),
            P("comp", None),
            P("comp", None),
            P("comp", None, "tp"),
            P(),
        ),
        out_specs=(
            P("comp", None, "tp"),
            P("comp", None, "tp"),
            P("comp", None),
            P("comp", None),
            P("comp", None, None),
            P("comp", None, None),
        ),
        check_vma=False,
    )
```

```python
import functools
import jax
import jax.numpy as jnp
from jax import lax
from jax.experimental import pallas as pl
from jax.experimental.pallas import tpu as pltpu
from jax.sharding import PartitionSpec as P

GROUP = 8
BLK = 64
QUAD = 4
COLS = 256
NEG = -1e30
VMEM = 60 * 1024 * 1024
MESH = pl.DeviceIdType.MESH


def contract(left, right, left_dim, right_dim):
    return lax.dot_general(
        left, right, (((left_dim,), (right_dim,)), ((), ())), preferred_element_type=jnp.float32
    )


def kernel(
    n, q_in, ka_in, va_in, kp_in, vp_in, do_in, cnt_in,
    att_out, dq_out, gp_out, ga_out,
    att_ref, dq_ref, gp_ref, ga_ref, gp_own, ga_own, q_ref, do_ref, cnt_ref, k_all, v_all, do_m, st, pb, dsb,
    nsend, nrecv, pown, psend, precv, aown, asend, arecv,
    pzown, pzsend, pzrecv,
    send_sem, recv_sem, load_sem,
):
    me = lax.axis_index("comp")
    tp = lax.axis_index("tp")
    local = lax.rem(tp, GROUP)
    base = tp - local
    length, hd = q_ref.shape
    shard = kp_in.shape[0]
    prompt = n * shard
    factor = hd ** (-0.5)
    blocks = length // COLS
    chips = n // 2
    core = lax.rem(me, 2)
    sibling = {"comp": me + 1 - 2 * core}
    chip_to = [None] + [{"comp": lax.rem(me + 2 * d, n)} for d in range(1, chips)]
    chip_back = [None] + [{"comp": lax.rem(me + n - 2 * d, n)} for d in range(1, chips)]
    octet = [None] + [{"tp": base + lax.rem(local + e, GROUP)} for e in range(1, GROUP)]

    barrier = pltpu.get_barrier_semaphore()
    peers = chip_to[1:] + [sibling] + octet[1:]
    for peer in peers:
        pl.semaphore_signal(barrier, inc=1, device_id=peer, device_id_type=MESH)

    loads = []
    for s, (src, dst) in enumerate((
        (kp_in, k_all.at[pl.ds(0, shard)]), (vp_in, v_all.at[pl.ds(0, shard)]),
        (ka_in, k_all.at[pl.ds(prompt, length)]), (q_in, q_ref), (cnt_in, cnt_ref), (do_in, do_ref),
        (va_in, v_all.at[pl.ds(prompt, length)]),
    )):
        loads.append(pltpu.make_async_copy(src, dst, load_sem.at[s]))
        loads[-1].start()

    count = [0]
    started = []

    def copy(src, dst, device):
        s = count[0]
        count[0] += 1
        c = pltpu.make_async_remote_copy(
            src_ref=src, dst_ref=dst, send_sem=send_sem.at[s], recv_sem=recv_sem.at[s],
            device_id=device, device_id_type=MESH,
        )
        started.append(c)
        return c

    pl.semaphore_wait(barrier, len(peers))

    def slot(ref, d, other):
        return ref.at[pl.ds((2 * d + other) * shard, shard)]

    def spread(ref):
        near = copy(slot(ref, 0, 0), slot(ref, 0, 1), sibling)
        far = [copy(slot(ref, 0, 0), slot(ref, d, 0), chip_to[d]) for d in range(1, chips)]
        for c in far + [near]:
            c.start()
        return near, far

    loads[0].wait()
    k_in = spread(k_all)
    loads[1].wait()
    v_in = spread(v_all)

    def forward(ref, far, d):
        far[d - 1].wait_recv()
        c = copy(slot(ref, d, 0), slot(ref, d, 1), sibling)
        c.start()
        return c

    def cols(b):
        return slice(b * COLS, (b + 1) * COLS)

    def spans(b):
        return [(d * shard, shard) for d in range(n)] + [(prompt + a * COLS, COLS) for a in range(b + 1)]

    peaks = [None] * blocks

    def scores(b, at, size):
        s = contract(k_all[at:at + size], q_ref[cols(b)], 1, 1) * factor
        if at == prompt + b * COLS:
            m = lax.broadcasted_iota(jnp.int32, s.shape, 0)
            i = lax.broadcasted_iota(jnp.int32, s.shape, 1)
            s = jnp.where(m <= i, s, NEG)
        st[at:at + size, cols(b)] = s
        top = jnp.max(s, axis=0, keepdims=True)
        peaks[b] = top if peaks[b] is None else jnp.maximum(peaks[b], top)

    for c in loads[2:4]:
        c.wait()
    for b in range(blocks):
        for a in range(b + 1):
            scores(b, prompt + a * COLS, COLS)
        scores(b, 0, shard)
    for c in loads[4:]:
        c.wait()
    own_count = cnt_ref[me] * BLK
    row = lax.broadcasted_iota(jnp.int32, (length, hd), 0)
    do_m[...] = jnp.where(row < own_count, do_ref[...].astype(jnp.float32), 0.0).astype(jnp.bfloat16)
    k_in[0].wait_recv()
    for b in range(blocks):
        scores(b, shard, shard)
    k_fwd = [forward(k_all, k_in[1], d) for d in range(1, chips)]
    for d in range(1, chips):
        for b in range(blocks):
            scores(b, 2 * d * shard, shard)
    v_fwd = [forward(v_all, v_in[1], d) for d in range(1, chips)]
    for d in range(1, chips):
        k_fwd[d - 1].wait_recv()
        for b in range(blocks):
            scores(b, (2 * d + 1) * shard, shard)

    for b in range(blocks):
        total = jnp.zeros((1, COLS), jnp.float32)
        for at, size in spans(b):
            e = jnp.exp(st[at:at + size, cols(b)] - peaks[b])
            st[at:at + size, cols(b)] = e
            total = total + jnp.sum(e, axis=0, keepdims=True)
        inv = 1.0 / total
        for at, size in spans(b):
            p = st[at:at + size, cols(b)] * inv
            st[at:at + size, cols(b)] = p
            pb[at:at + size, cols(b)] = p.astype(jnp.bfloat16)

    p_near, p_far = [None, None], [None, None]

    def prompt_terms(w, probs, right):
        for slot_i in [2 * d + 1 for d in range(chips)] + [2 * d for d in range(chips)]:
            g = jnp.dot(
                probs[slot_i * shard:(slot_i + 1) * shard], right[...], preferred_element_type=jnp.float32
            )
            if slot_i % 2:
                nsend[w, slot_i // 2] = g.astype(jnp.bfloat16)
                if slot_i // 2 == chips - 1:
                    p_near[w] = copy(nsend.at[w], nrecv.at[w], sibling)
                    p_near[w].start()
            else:
                pown[w, slot_i // 2] = g

    def prompt_far(w):
        p_near[w].wait_recv()
        p_far[w] = []
        for d in range(1, chips):
            psend[w, d - 1] = (pown[w, d] + nrecv[w, d].astype(jnp.float32)).astype(jnp.bfloat16)
            p_far[w].append(copy(psend.at[w, d - 1], precv.at[w, d - 1], chip_back[d]))
            p_far[w][-1].start()

    def octet_scatter(send, recv, place):
        out = []
        for e in range(1, GROUP):
            out.append(copy(send.at[place(lax.rem(local + e, GROUP))], recv.at[e - 1], octet[e]))
            out[-1].start()
        return out

    def octet_gather(copies, own, recv, stage, out, place):
        total = own[place(local)]
        for e in range(1, GROUP):
            copies[e - 1].wait_recv()
            total = total + recv[e - 1].astype(jnp.float32)
        stage[...] = total.astype(jnp.bfloat16)
        first = count[0]
        for e in range(1, GROUP):
            copy(stage, out.at[place(local)], octet[e]).start()
        out[place(local)] = total.astype(jnp.bfloat16)
        return first

    def octet_finish(first, out, place):
        for e in range(1, GROUP):
            ref = out.at[place(lax.rem(local + GROUP - e, GROUP))]
            pltpu.make_async_remote_copy(
                src_ref=ref, dst_ref=ref, send_sem=send_sem.at[first + e - 1], recv_sem=recv_sem.at[first + e - 1],
                device_id=octet[e], device_id_type=MESH,
            ).wait_recv()

    def straight(member):
        return member

    def paired(member):
        return lax.rem(member, 2) * QUAD + member // 2

    eighth = length // GROUP

    def answer_terms(w, probs, right):
        for a in range(blocks):
            at = prompt + a * COLS
            g = jnp.dot(
                probs[at:at + COLS, a * COLS:], right[a * COLS:], preferred_element_type=jnp.float32
            ).reshape(COLS // eighth, eighth, hd)
            first = a * COLS // eighth
            aown[w, first:first + COLS // eighth] = g
            asend[w, first:first + COLS // eighth] = g.astype(jnp.bfloat16)
        return octet_scatter(asend.at[w], arecv.at[w], straight)

    prompt_terms(1, pb, do_m)
    av = answer_terms(1, pb, do_m)

    prompt_far(1)
    for c in [v_in[0]] + v_fwd:
        c.wait_recv()
    stores = []

    def keep(src, dst):
        stores.append(pltpu.make_async_copy(src, dst, load_sem.at[7 + len(stores)]))
        stores[-1].start()

    deltas = []
    for b in range(blocks):
        keys = prompt + (b + 1) * COLS
        mixed = contract(v_all[:keys], pb[:keys, cols(b)], 0, 0)
        lane = lax.broadcasted_iota(jnp.int32, mixed.shape, 1) + b * COLS
        mixed = jnp.where(lane < own_count, mixed, 0.0).astype(jnp.bfloat16).astype(jnp.float32)
        att_ref[cols(b)] = mixed.T.astype(jnp.bfloat16)
        dout_t = do_m[cols(b)].astype(jnp.float32).T
        deltas.append(jnp.sum(dout_t * mixed, axis=0, keepdims=True))

    keep(att_ref, att_out)
    def score_grads(b, at, size):
        dp = contract(v_all[at:at + size], do_m[cols(b)], 1, 1)
        ds = st[at:at + size, cols(b)] * (dp - deltas[b]) * factor
        dsb[at:at + size, cols(b)] = ds.astype(jnp.bfloat16)

    for b in range(blocks):
        for at, size in spans(b)[:n]:
            score_grads(b, at, size)
    prompt_terms(0, dsb, q_ref)
    for b in range(blocks):
        for at, size in spans(b)[n:]:
            score_grads(b, at, size)
    ak = answer_terms(0, dsb, q_ref)
    prompt_far(0)
    av_out = octet_gather(av, aown.at[1], arecv.at[1], ga_own.at[1], ga_ref.at[1], straight)

    for b in range(blocks):
        keys = prompt + (b + 1) * COLS
        dq = contract(k_all[:keys], dsb[:keys, cols(b)], 0, 0)
        dq_ref[cols(b)] = dq.T.astype(jnp.bfloat16)
    keep(dq_ref, dq_out)

    for w in (1, 0):
        total = pown[w, 0] + nrecv[w, 0].astype(jnp.float32)
        for d in range(1, chips):
            p_far[w][d - 1].wait_recv()
            total = total + precv[w, d - 1].astype(jnp.float32)
        size = shard // QUAD
        for z in range(QUAD):
            pzown[w * QUAD + z] = total[z * size:(z + 1) * size]
            pzsend[w * QUAD + z] = total[z * size:(z + 1) * size].astype(jnp.bfloat16)

    ap = octet_scatter(pzsend, pzrecv, paired)
    ak_out = octet_gather(ak, aown.at[0], arecv.at[0], ga_own.at[0], ga_ref.at[0], straight)
    ap_out = octet_gather(ap, pzown, pzrecv, gp_own, gp_ref, paired)
    octet_finish(av_out, ga_ref.at[1], straight)
    keep(ga_ref.at[1], ga_out.at[1])
    octet_finish(ak_out, ga_ref.at[0], straight)
    keep(ga_ref.at[0], ga_out.at[0])
    octet_finish(ap_out, gp_ref, paired)
    keep(gp_ref, gp_out)
    for c in stores:
        c.wait()
    for c in started:
        c.wait_send()


def fused(queries, answer_keys, answer_values, prompt_keys, prompt_values, out_grad, block_counts, n):
    length, hd = queries.shape
    shard = prompt_keys.shape[0]
    keys = n * shard + length
    eighth = length // GROUP
    piece = shard // QUAD
    bf, f32 = jnp.bfloat16, jnp.float32
    chips = n // 2
    sems = 2 * (2 * chips - 1) + 2 * chips + 6 * (GROUP - 1)
    hbm = pl.BlockSpec(memory_space=pl.ANY)
    return pl.pallas_call(
        functools.partial(kernel, n),
        out_shape=(
            jax.ShapeDtypeStruct((length, hd), bf),
            jax.ShapeDtypeStruct((length, hd), bf),
            jax.ShapeDtypeStruct((GROUP, piece, hd), bf),
            jax.ShapeDtypeStruct((2, GROUP, eighth, hd), bf),
        ),
        in_specs=[hbm] * 7,
        out_specs=(hbm,) * 4,
        scratch_shapes=[
            pltpu.VMEM((length, hd), bf),
            pltpu.VMEM((length, hd), bf),
            pltpu.VMEM((GROUP, piece, hd), bf),
            pltpu.VMEM((2, GROUP, eighth, hd), bf),
            pltpu.VMEM((piece, hd), bf),
            pltpu.VMEM((2, eighth, hd), bf),
            pltpu.VMEM((length, hd), bf),
            pltpu.VMEM((length, hd), bf),
            pltpu.SMEM(block_counts.shape, jnp.int32),
            pltpu.VMEM((keys, hd), bf),
            pltpu.VMEM((keys, hd), bf),
            pltpu.VMEM((length, hd), bf),
            pltpu.VMEM((keys, length), f32),
            pltpu.VMEM((keys, length), bf),
            pltpu.VMEM((keys, length), bf),
            pltpu.VMEM((2, chips, shard, hd), bf),
            pltpu.VMEM((2, chips, shard, hd), bf),
            pltpu.VMEM((2, chips, shard, hd), f32),
            pltpu.VMEM((2, chips - 1, shard, hd), bf),
            pltpu.VMEM((2, chips - 1, shard, hd), bf),
            pltpu.VMEM((2, GROUP, eighth, hd), f32),
            pltpu.VMEM((2, GROUP, eighth, hd), bf),
            pltpu.VMEM((2, GROUP - 1, eighth, hd), bf),
            pltpu.VMEM((GROUP, piece, hd), f32),
            pltpu.VMEM((GROUP, piece, hd), bf),
            pltpu.VMEM((GROUP - 1, piece, hd), bf),
            pltpu.SemaphoreType.DMA((sems,)),
            pltpu.SemaphoreType.DMA((sems,)),
            pltpu.SemaphoreType.DMA((12,)),
        ],
        compiler_params=pltpu.CompilerParams(
            collective_id=0, has_side_effects=True, vmem_limit_bytes=VMEM
        ),
    )(queries, answer_keys, answer_values, prompt_keys, prompt_values, out_grad, block_counts)


def store(att, dq, gp, ga, *refs):
    outs, held, load, save = refs[:6], refs[6:12], refs[12], refs[13]
    sources = (ga.at[0], ga.at[1], att, dq, gp.at[0], gp.at[1])
    copies = [
        (pltpu.make_async_copy(src, mid, load.at[s]), pltpu.make_async_copy(mid, dst, save.at[s]))
        for s, (src, mid, dst) in enumerate(zip(sources, held, outs))
    ]
    for c, _ in copies:
        c.start()
    for c, then in copies:
        c.wait()
        then.start()
    for _, c in copies:
        c.wait()


def write_out(att, dq, gp, ga):
    shapes = [jax.ShapeDtypeStruct(x.shape, x.dtype) for x in (ga[0], ga[1], att, dq, gp[0], gp[1])]
    results = pl.pallas_call(
        store,
        out_shape=shapes,
        in_specs=[pl.BlockSpec(memory_space=pl.ANY)] * 4,
        out_specs=[pl.BlockSpec(memory_space=pl.ANY)] * 6,
        scratch_shapes=[pltpu.VMEM(x.shape, x.dtype) for x in shapes]
        + [pltpu.SemaphoreType.DMA((6,)), pltpu.SemaphoreType.DMA((6,))],
        compiler_params=pltpu.CompilerParams(vmem_limit_bytes=VMEM),
    )(att, dq, gp, ga)
    return results[2], results[3], results[4:], results[:2]


def shards(n, groups, queries, answer_keys, answer_values, prompt_keys, prompt_values, out_grad, block_counts):
    hd = queries.shape[2]
    length = queries.shape[1]
    shard = prompt_keys.shape[0]
    kv = [answer_keys[0], answer_values[0], prompt_keys, prompt_values]
    if groups > 1:
        kv_group = lax.axis_index("tp") // GROUP
        kv = [lax.dynamic_slice_in_dim(x, kv_group * hd, hd, 1) for x in kv]
    attended, query_grad, gp, ga = fused(queries[0], *kv, out_grad[0], block_counts, n)
    gp = gp.reshape(2, shard, hd)
    attended, query_grad, gp, ga = write_out(attended, query_grad, gp, ga)
    outs = [gp[0].reshape(shard, hd), gp[1].reshape(shard, hd), ga[0].reshape(length, hd), ga[1].reshape(length, hd)]
    if groups > 1:
        sets = [[g * GROUP + i for g in range(groups)] for i in range(GROUP)]
        outs = [lax.all_gather(x, "tp", axis=1, tiled=True, axis_index_groups=sets) for x in outs]
    return attended[None], query_grad[None], outs[0], outs[1], outs[2][None], outs[3][None]


def solution(mesh):
    n, tp = mesh.shape["comp"], mesh.shape["tp"]
    return jax.shard_map(
        functools.partial(shards, n, tp // GROUP),
        mesh=mesh,
        in_specs=(
            P("comp", None, "tp"),
            P("comp", None, None),
            P("comp", None, None),
            P("comp", None),
            P("comp", None),
            P("comp", None, "tp"),
            P(),
        ),
        out_specs=(
            P("comp", None, "tp"),
            P("comp", None, "tp"),
            P("comp", None),
            P("comp", None),
            P("comp", None, None),
            P("comp", None, None),
        ),
        check_vma=False,
    )
```

```python
import functools
import jax
import jax.numpy as jnp
from jax import lax
from jax.experimental import pallas as pl
from jax.experimental.pallas import tpu as pltpu
from jax.sharding import PartitionSpec as P

GROUP = 8
BLK = 64
QUAD = 4
COLS = 256
NEG = -1e30
VMEM = 60 * 1024 * 1024
MESH = pl.DeviceIdType.MESH


def contract(left, right, left_dim, right_dim):
    return lax.dot_general(
        left, right, (((left_dim,), (right_dim,)), ((), ())), preferred_element_type=jnp.float32
    )


def kernel(
    n, q_in, ka_in, va_in, kp_in, vp_in, do_in, cnt_in,
    att_out, dq_out, gp_out, ga_out,
    att_ref, dq_ref, gp_ref, ga_ref, gp_own, ga_own, q_ref, do_ref, cnt_ref, k_all, v_all, do_m, st, pb, dsb,
    nsend, nrecv, pown, psend, precv, aown, asend, arecv,
    pzown, pzsend, pzrecv,
    send_sem, recv_sem, load_sem,
):
    me = lax.axis_index("comp")
    tp = lax.axis_index("tp")
    local = lax.rem(tp, GROUP)
    base = tp - local
    other = local + 1 - 2 * lax.rem(local, 2)
    partner = {"tp": base + other}
    length, hd = q_ref.shape
    shard = kp_in.shape[0]
    prompt = n * shard
    factor = hd ** (-0.5)
    blocks = length // COLS
    chips = n // 2
    core = lax.rem(me, 2)
    sibling = {"comp": me + 1 - 2 * core}
    chip_to = [None] + [{"comp": lax.rem(me + 2 * d, n)} for d in range(1, chips)]
    chip_back = [None] + [{"comp": lax.rem(me + n - 2 * d, n)} for d in range(1, chips)]
    octet = [None] + [{"tp": base + lax.rem(local + e, GROUP)} for e in range(1, GROUP)]

    barrier = pltpu.get_barrier_semaphore()
    peers = chip_to[1:] + [sibling] + octet[1:]
    for peer in peers:
        pl.semaphore_signal(barrier, inc=1, device_id=peer, device_id_type=MESH)

    loads = []
    for s, (src, dst) in enumerate((
        (kp_in, k_all.at[pl.ds(0, shard)]), (vp_in, v_all.at[pl.ds(0, shard)]),
        (ka_in, k_all.at[pl.ds(prompt, length)]), (q_in, q_ref), (cnt_in, cnt_ref), (do_in, do_ref),
        (va_in, v_all.at[pl.ds(prompt, length)]),
    )):
        loads.append(pltpu.make_async_copy(src, dst, load_sem.at[s]))
        loads[-1].start()

    count = [0]
    started = []

    def copy(src, dst, device):
        s = count[0]
        count[0] += 1
        c = pltpu.make_async_remote_copy(
            src_ref=src, dst_ref=dst, send_sem=send_sem.at[s], recv_sem=recv_sem.at[s],
            device_id=device, device_id_type=MESH,
        )
        started.append(c)
        return c

    pl.semaphore_wait(barrier, len(peers))

    def slot(ref, d, other):
        return ref.at[pl.ds((2 * d + other) * shard, shard)]

    def spread(ref):
        near = copy(slot(ref, 0, 0), slot(ref, 0, 1), sibling)
        far = [copy(slot(ref, 0, 0), slot(ref, d, 0), chip_to[d]) for d in range(1, chips)]
        for c in far + [near]:
            c.start()
        return near, far

    loads[0].wait()
    k_in = spread(k_all)
    loads[1].wait()
    v_in = spread(v_all)

    def forward(ref, far, d):
        far[d - 1].wait_recv()
        c = copy(slot(ref, d, 0), slot(ref, d, 1), sibling)
        c.start()
        return c

    def cols(b):
        return slice(b * COLS, (b + 1) * COLS)

    def spans(b):
        return [(d * shard, shard) for d in range(n)] + [(prompt + a * COLS, COLS) for a in range(b + 1)]

    peaks = [None] * blocks

    def scores(b, at, size):
        s = contract(k_all[at:at + size], q_ref[cols(b)], 1, 1) * factor
        if at == prompt + b * COLS:
            m = lax.broadcasted_iota(jnp.int32, s.shape, 0)
            i = lax.broadcasted_iota(jnp.int32, s.shape, 1)
            s = jnp.where(m <= i, s, NEG)
        st[at:at + size, cols(b)] = s
        top = jnp.max(s, axis=0, keepdims=True)
        peaks[b] = top if peaks[b] is None else jnp.maximum(peaks[b], top)

    for c in loads[2:4]:
        c.wait()
    for b in range(blocks):
        for a in range(b + 1):
            scores(b, prompt + a * COLS, COLS)
        scores(b, 0, shard)
    for c in loads[4:]:
        c.wait()
    own_count = cnt_ref[me] * BLK
    row = lax.broadcasted_iota(jnp.int32, (length, hd), 0)
    do_m[...] = jnp.where(row < own_count, do_ref[...].astype(jnp.float32), 0.0).astype(jnp.bfloat16)
    k_in[0].wait_recv()
    for b in range(blocks):
        scores(b, shard, shard)
    k_fwd = [forward(k_all, k_in[1], d) for d in range(1, chips)]
    for d in range(1, chips):
        for b in range(blocks):
            scores(b, 2 * d * shard, shard)
    v_fwd = [forward(v_all, v_in[1], d) for d in range(1, chips)]
    for d in range(1, chips):
        k_fwd[d - 1].wait_recv()
        for b in range(blocks):
            scores(b, (2 * d + 1) * shard, shard)

    for b in range(blocks):
        total = jnp.zeros((1, COLS), jnp.float32)
        for at, size in spans(b):
            e = jnp.exp(st[at:at + size, cols(b)] - peaks[b])
            st[at:at + size, cols(b)] = e
            total = total + jnp.sum(e, axis=0, keepdims=True)
        inv = 1.0 / total
        for at, size in spans(b):
            p = st[at:at + size, cols(b)] * inv
            st[at:at + size, cols(b)] = p
            pb[at:at + size, cols(b)] = p.astype(jnp.bfloat16)

    p_near, p_far = [None, None], [None, None]

    def prompt_terms(w, probs, right):
        for slot_i in [2 * d + 1 for d in range(chips)] + [2 * d for d in range(chips)]:
            g = jnp.dot(
                probs[slot_i * shard:(slot_i + 1) * shard], right[...], preferred_element_type=jnp.float32
            )
            if slot_i % 2:
                nsend[w, slot_i // 2] = g.astype(jnp.bfloat16)
                if slot_i // 2 == chips - 1:
                    p_near[w] = copy(nsend.at[w], nrecv.at[w], sibling)
                    p_near[w].start()
            else:
                pown[w, slot_i // 2] = g

    def prompt_far(w):
        p_near[w].wait_recv()
        p_far[w] = []
        for d in range(1, chips):
            psend[w, d - 1] = (pown[w, d] + nrecv[w, d].astype(jnp.float32)).astype(jnp.bfloat16)
            p_far[w].append(copy(psend.at[w, d - 1], precv.at[w, d - 1], chip_back[d]))
            p_far[w][-1].start()

    def octet_scatter(send, recv, place):
        out = []
        for e in range(1, GROUP):
            out.append(copy(send.at[place(lax.rem(local + e, GROUP))], recv.at[e - 1], octet[e]))
            out[-1].start()
        return out

    def octet_gather(copies, own, recv, stage, out, place):
        total = own[place(local)]
        for e in range(1, GROUP):
            copies[e - 1].wait_recv()
            total = total + recv[e - 1].astype(jnp.float32)
        stage[...] = total.astype(jnp.bfloat16)
        first = count[0]
        for e in range(1, GROUP):
            copy(stage, out.at[place(local)], octet[e]).start()
        out[place(local)] = total.astype(jnp.bfloat16)
        return first

    def octet_finish(first, out, place):
        for e in range(1, GROUP):
            ref = out.at[place(lax.rem(local + GROUP - e, GROUP))]
            pltpu.make_async_remote_copy(
                src_ref=ref, dst_ref=ref, send_sem=send_sem.at[first + e - 1], recv_sem=recv_sem.at[first + e - 1],
                device_id=octet[e], device_id_type=MESH,
            ).wait_recv()

    def relay_gather(copies, own, recv, stage, out):
        total = own[local]
        for e in range(1, GROUP):
            copies[e - 1].wait_recv()
            total = total + recv[e - 1].astype(jnp.float32)
        stage[...] = total.astype(jnp.bfloat16)
        first = count[0]
        for e in range(2, GROUP, 2):
            copy(stage, out.at[local], octet[e]).start()
        copy(stage, out.at[local], partner).start()
        out[local] = total.astype(jnp.bfloat16)
        return first

    def arrived(s, ref):
        pltpu.make_async_remote_copy(
            src_ref=ref, dst_ref=ref, send_sem=send_sem.at[s], recv_sem=recv_sem.at[s],
            device_id=partner, device_id_type=MESH,
        ).wait_recv()

    def relay_forward(first, out):
        passed = [first + QUAD - 1]
        for z in range(1, QUAD):
            piece = out.at[lax.rem(local + GROUP - 2 * z, GROUP)]
            arrived(first + z - 1, piece)
            passed.append(count[0])
            copy(piece, piece, partner).start()
        return passed

    def relay_finish(passed, out):
        for z in range(QUAD):
            arrived(passed[z], out.at[lax.rem(other + GROUP - 2 * z, GROUP)])

    def straight(member):
        return member

    def paired(member):
        return lax.rem(member, 2) * QUAD + member // 2

    eighth = length // GROUP

    def answer_terms(w, probs, right):
        for a in range(blocks):
            at = prompt + a * COLS
            g = jnp.dot(
                probs[at:at + COLS, a * COLS:], right[a * COLS:], preferred_element_type=jnp.float32
            ).reshape(COLS // eighth, eighth, hd)
            first = a * COLS // eighth
            aown[w, first:first + COLS // eighth] = g
            asend[w, first:first + COLS // eighth] = g.astype(jnp.bfloat16)
        return octet_scatter(asend.at[w], arecv.at[w], straight)

    prompt_terms(1, pb, do_m)
    av = answer_terms(1, pb, do_m)

    prompt_far(1)
    for c in [v_in[0]] + v_fwd:
        c.wait_recv()
    stores = []

    def keep(src, dst):
        stores.append(pltpu.make_async_copy(src, dst, load_sem.at[7 + len(stores)]))
        stores[-1].start()

    deltas = []
    for b in range(blocks):
        keys = prompt + (b + 1) * COLS
        mixed = contract(v_all[:keys], pb[:keys, cols(b)], 0, 0)
        lane = lax.broadcasted_iota(jnp.int32, mixed.shape, 1) + b * COLS
        mixed = jnp.where(lane < own_count, mixed, 0.0).astype(jnp.bfloat16).astype(jnp.float32)
        att_ref[cols(b)] = mixed.T.astype(jnp.bfloat16)
        dout_t = do_m[cols(b)].astype(jnp.float32).T
        deltas.append(jnp.sum(dout_t * mixed, axis=0, keepdims=True))

    keep(att_ref, att_out)
    def score_grads(b, at, size):
        dp = contract(v_all[at:at + size], do_m[cols(b)], 1, 1)
        ds = st[at:at + size, cols(b)] * (dp - deltas[b]) * factor
        dsb[at:at + size, cols(b)] = ds.astype(jnp.bfloat16)

    for b in range(blocks):
        for at, size in spans(b)[:n]:
            score_grads(b, at, size)
    prompt_terms(0, dsb, q_ref)
    for b in range(blocks):
        for at, size in spans(b)[n:]:
            score_grads(b, at, size)
    prompt_far(0)
    ak = answer_terms(0, dsb, q_ref)
    av_out = relay_gather(av, aown.at[1], arecv.at[1], ga_own.at[1], ga_ref.at[1])

    for b in range(blocks):
        keys = prompt + (b + 1) * COLS
        dq = contract(k_all[:keys], dsb[:keys, cols(b)], 0, 0)
        dq_ref[cols(b)] = dq.T.astype(jnp.bfloat16)
    keep(dq_ref, dq_out)

    for w in (1, 0):
        total = pown[w, 0] + nrecv[w, 0].astype(jnp.float32)
        for d in range(1, chips):
            p_far[w][d - 1].wait_recv()
            total = total + precv[w, d - 1].astype(jnp.float32)
        size = shard // QUAD
        for z in range(QUAD):
            pzown[w * QUAD + z] = total[z * size:(z + 1) * size]
            pzsend[w * QUAD + z] = total[z * size:(z + 1) * size].astype(jnp.bfloat16)

    ap = octet_scatter(pzsend, pzrecv, paired)
    av_out = relay_forward(av_out, ga_ref.at[1])
    ak_out = relay_gather(ak, aown.at[0], arecv.at[0], ga_own.at[0], ga_ref.at[0])
    ap_out = octet_gather(ap, pzown, pzrecv, gp_own, gp_ref, paired)
    ak_out = relay_forward(ak_out, ga_ref.at[0])
    relay_finish(av_out, ga_ref.at[1])
    keep(ga_ref.at[1], ga_out.at[1])
    relay_finish(ak_out, ga_ref.at[0])
    keep(ga_ref.at[0], ga_out.at[0])
    octet_finish(ap_out, gp_ref, paired)
    keep(gp_ref, gp_out)
    for c in stores:
        c.wait()
    for c in started:
        c.wait_send()


def fused(queries, answer_keys, answer_values, prompt_keys, prompt_values, out_grad, block_counts, n):
    length, hd = queries.shape
    shard = prompt_keys.shape[0]
    keys = n * shard + length
    eighth = length // GROUP
    piece = shard // QUAD
    bf, f32 = jnp.bfloat16, jnp.float32
    chips = n // 2
    sems = 2 * (2 * chips - 1) + 2 * chips + 6 * (GROUP - 1)
    hbm = pl.BlockSpec(memory_space=pl.ANY)
    return pl.pallas_call(
        functools.partial(kernel, n),
        out_shape=(
            jax.ShapeDtypeStruct((length, hd), bf),
            jax.ShapeDtypeStruct((length, hd), bf),
            jax.ShapeDtypeStruct((GROUP, piece, hd), bf),
            jax.ShapeDtypeStruct((2, GROUP, eighth, hd), bf),
        ),
        in_specs=[hbm] * 7,
        out_specs=(hbm,) * 4,
        scratch_shapes=[
            pltpu.VMEM((length, hd), bf),
            pltpu.VMEM((length, hd), bf),
            pltpu.VMEM((GROUP, piece, hd), bf),
            pltpu.VMEM((2, GROUP, eighth, hd), bf),
            pltpu.VMEM((piece, hd), bf),
            pltpu.VMEM((2, eighth, hd), bf),
            pltpu.VMEM((length, hd), bf),
            pltpu.VMEM((length, hd), bf),
            pltpu.SMEM(block_counts.shape, jnp.int32),
            pltpu.VMEM((keys, hd), bf),
            pltpu.VMEM((keys, hd), bf),
            pltpu.VMEM((length, hd), bf),
            pltpu.VMEM((keys, length), f32),
            pltpu.VMEM((keys, length), bf),
            pltpu.VMEM((keys, length), bf),
            pltpu.VMEM((2, chips, shard, hd), bf),
            pltpu.VMEM((2, chips, shard, hd), bf),
            pltpu.VMEM((2, chips, shard, hd), f32),
            pltpu.VMEM((2, chips - 1, shard, hd), bf),
            pltpu.VMEM((2, chips - 1, shard, hd), bf),
            pltpu.VMEM((2, GROUP, eighth, hd), f32),
            pltpu.VMEM((2, GROUP, eighth, hd), bf),
            pltpu.VMEM((2, GROUP - 1, eighth, hd), bf),
            pltpu.VMEM((GROUP, piece, hd), f32),
            pltpu.VMEM((GROUP, piece, hd), bf),
            pltpu.VMEM((GROUP - 1, piece, hd), bf),
            pltpu.SemaphoreType.DMA((sems,)),
            pltpu.SemaphoreType.DMA((sems,)),
            pltpu.SemaphoreType.DMA((12,)),
        ],
        compiler_params=pltpu.CompilerParams(
            collective_id=0, has_side_effects=True, vmem_limit_bytes=VMEM
        ),
    )(queries, answer_keys, answer_values, prompt_keys, prompt_values, out_grad, block_counts)


def store(att, dq, gp, ga, *refs):
    outs, held, load, save = refs[:6], refs[6:12], refs[12], refs[13]
    sources = (ga.at[0], ga.at[1], att, dq, gp.at[0], gp.at[1])
    copies = [
        (pltpu.make_async_copy(src, mid, load.at[s]), pltpu.make_async_copy(mid, dst, save.at[s]))
        for s, (src, mid, dst) in enumerate(zip(sources, held, outs))
    ]
    for c, _ in copies:
        c.start()
    for c, then in copies:
        c.wait()
        then.start()
    for _, c in copies:
        c.wait()


def write_out(att, dq, gp, ga):
    shapes = [jax.ShapeDtypeStruct(x.shape, x.dtype) for x in (ga[0], ga[1], att, dq, gp[0], gp[1])]
    results = pl.pallas_call(
        store,
        out_shape=shapes,
        in_specs=[pl.BlockSpec(memory_space=pl.ANY)] * 4,
        out_specs=[pl.BlockSpec(memory_space=pl.ANY)] * 6,
        scratch_shapes=[pltpu.VMEM(x.shape, x.dtype) for x in shapes]
        + [pltpu.SemaphoreType.DMA((6,)), pltpu.SemaphoreType.DMA((6,))],
        compiler_params=pltpu.CompilerParams(vmem_limit_bytes=VMEM),
    )(att, dq, gp, ga)
    return results[2], results[3], results[4:], results[:2]


def shards(n, groups, queries, answer_keys, answer_values, prompt_keys, prompt_values, out_grad, block_counts):
    hd = queries.shape[2]
    length = queries.shape[1]
    shard = prompt_keys.shape[0]
    kv = [answer_keys[0], answer_values[0], prompt_keys, prompt_values]
    if groups > 1:
        kv_group = lax.axis_index("tp") // GROUP
        kv = [lax.dynamic_slice_in_dim(x, kv_group * hd, hd, 1) for x in kv]
    attended, query_grad, gp, ga = fused(queries[0], *kv, out_grad[0], block_counts, n)
    gp = gp.reshape(2, shard, hd)
    attended, query_grad, gp, ga = write_out(attended, query_grad, gp, ga)
    outs = [gp[0].reshape(shard, hd), gp[1].reshape(shard, hd), ga[0].reshape(length, hd), ga[1].reshape(length, hd)]
    if groups > 1:
        sets = [[g * GROUP + i for g in range(groups)] for i in range(GROUP)]
        outs = [lax.all_gather(x, "tp", axis=1, tiled=True, axis_index_groups=sets) for x in outs]
    return attended[None], query_grad[None], outs[0], outs[1], outs[2][None], outs[3][None]


def solution(mesh):
    n, tp = mesh.shape["comp"], mesh.shape["tp"]
    return jax.shard_map(
        functools.partial(shards, n, tp // GROUP),
        mesh=mesh,
        in_specs=(
            P("comp", None, "tp"),
            P("comp", None, None),
            P("comp", None, None),
            P("comp", None),
            P("comp", None),
            P("comp", None, "tp"),
            P(),
        ),
        out_specs=(
            P("comp", None, "tp"),
            P("comp", None, "tp"),
            P("comp", None),
            P("comp", None),
            P("comp", None, None),
            P("comp", None, None),
        ),
        check_vma=False,
    )
```

```python
import functools
import jax
import jax.numpy as jnp
from jax import lax
from jax.experimental import pallas as pl
from jax.experimental.pallas import tpu as pltpu
from jax.sharding import PartitionSpec as P

GROUP = 8
BLK = 64
QUAD = 4
COLS = 256
NEG = -1e30
VMEM = 60 * 1024 * 1024
MESH = pl.DeviceIdType.MESH


def contract(left, right, left_dim, right_dim):
    return lax.dot_general(
        left, right, (((left_dim,), (right_dim,)), ((), ())), preferred_element_type=jnp.float32
    )


def kernel(
    n, q_in, ka_in, va_in, kp_in, vp_in, do_in, cnt_in,
    att_out, dq_out, gp_out, ga_out,
    att_ref, dq_ref, gp_ref, ga_ref, gp_own, ga_own, q_ref, do_ref, cnt_ref, k_all, v_all, do_m, st, pb, dsb,
    nsend, nrecv, pown, psend, precv, aown, asend, arecv,
    pzown, pzsend, pzrecv,
    send_sem, recv_sem, load_sem,
):
    me = lax.axis_index("comp")
    tp = lax.axis_index("tp")
    local = lax.rem(tp, GROUP)
    base = tp - local
    other = local + 1 - 2 * lax.rem(local, 2)
    partner = {"tp": base + other}
    length, hd = q_ref.shape
    shard = kp_in.shape[0]
    prompt = n * shard
    factor = hd ** (-0.5)
    blocks = length // COLS
    chips = n // 2
    core = lax.rem(me, 2)
    sibling = {"comp": me + 1 - 2 * core}
    chip_to = [None] + [{"comp": lax.rem(me + 2 * d, n)} for d in range(1, chips)]
    chip_back = [None] + [{"comp": lax.rem(me + n - 2 * d, n)} for d in range(1, chips)]
    octet = [None] + [{"tp": base + lax.rem(local + e, GROUP)} for e in range(1, GROUP)]

    barrier = pltpu.get_barrier_semaphore()
    peers = chip_to[1:] + [sibling] + octet[1:]
    for peer in peers:
        pl.semaphore_signal(barrier, inc=1, device_id=peer, device_id_type=MESH)

    loads = []
    for s, (src, dst) in enumerate((
        (kp_in, k_all.at[pl.ds(0, shard)]), (vp_in, v_all.at[pl.ds(0, shard)]),
        (ka_in, k_all.at[pl.ds(prompt, length)]), (q_in, q_ref), (cnt_in, cnt_ref), (do_in, do_ref),
        (va_in, v_all.at[pl.ds(prompt, length)]),
    )):
        loads.append(pltpu.make_async_copy(src, dst, load_sem.at[s]))
        loads[-1].start()

    count = [0]
    started = []

    def copy(src, dst, device):
        s = count[0]
        count[0] += 1
        c = pltpu.make_async_remote_copy(
            src_ref=src, dst_ref=dst, send_sem=send_sem.at[s], recv_sem=recv_sem.at[s],
            device_id=device, device_id_type=MESH,
        )
        started.append(c)
        return c

    pl.semaphore_wait(barrier, len(peers))

    def slot(ref, d, other):
        return ref.at[pl.ds((2 * d + other) * shard, shard)]

    def spread(ref):
        near = copy(slot(ref, 0, 0), slot(ref, 0, 1), sibling)
        far = [copy(slot(ref, 0, 0), slot(ref, d, 0), chip_to[d]) for d in range(1, chips)]
        for c in far + [near]:
            c.start()
        return near, far

    loads[0].wait()
    k_in = spread(k_all)
    loads[1].wait()
    v_in = spread(v_all)

    def forward(ref, far, d):
        far[d - 1].wait_recv()
        c = copy(slot(ref, d, 0), slot(ref, d, 1), sibling)
        c.start()
        return c

    def cols(b):
        return slice(b * COLS, (b + 1) * COLS)

    def spans(b):
        return [(d * shard, shard) for d in range(n)] + [(prompt + a * COLS, COLS) for a in range(b + 1)]

    peaks = [None] * blocks

    def scores(b, at, size):
        s = contract(k_all[at:at + size], q_ref[cols(b)], 1, 1) * factor
        if at == prompt + b * COLS:
            m = lax.broadcasted_iota(jnp.int32, s.shape, 0)
            i = lax.broadcasted_iota(jnp.int32, s.shape, 1)
            s = jnp.where(m <= i, s, NEG)
        st[at:at + size, cols(b)] = s
        top = jnp.max(s, axis=0, keepdims=True)
        peaks[b] = top if peaks[b] is None else jnp.maximum(peaks[b], top)

    for c in loads[2:4]:
        c.wait()
    for b in range(blocks):
        for a in range(b + 1):
            scores(b, prompt + a * COLS, COLS)
        scores(b, 0, shard)
    for c in loads[4:]:
        c.wait()
    own_count = cnt_ref[me] * BLK
    row = lax.broadcasted_iota(jnp.int32, (length, hd), 0)
    do_m[...] = jnp.where(row < own_count, do_ref[...].astype(jnp.float32), 0.0).astype(jnp.bfloat16)
    k_in[0].wait_recv()
    for b in range(blocks):
        scores(b, shard, shard)
    k_fwd = [forward(k_all, k_in[1], d) for d in range(1, chips)]
    for d in range(1, chips):
        for b in range(blocks):
            scores(b, 2 * d * shard, shard)
    v_fwd = [forward(v_all, v_in[1], d) for d in range(1, chips)]
    for d in range(1, chips):
        k_fwd[d - 1].wait_recv()
        for b in range(blocks):
            scores(b, (2 * d + 1) * shard, shard)

    for b in range(blocks):
        total = jnp.zeros((1, COLS), jnp.float32)
        for at, size in spans(b):
            e = jnp.exp(st[at:at + size, cols(b)] - peaks[b])
            st[at:at + size, cols(b)] = e
            total = total + jnp.sum(e, axis=0, keepdims=True)
        inv = 1.0 / total
        for at, size in spans(b):
            p = st[at:at + size, cols(b)] * inv
            st[at:at + size, cols(b)] = p
            pb[at:at + size, cols(b)] = p.astype(jnp.bfloat16)

    p_near, p_far = [[None] * chips, [None] * chips], [None, None]

    def prompt_terms(w, probs, right):
        for slot_i in [2 * d + 1 for d in reversed(range(chips))] + [2 * d for d in reversed(range(chips))]:
            g = jnp.dot(
                probs[slot_i * shard:(slot_i + 1) * shard], right[...], preferred_element_type=jnp.float32
            )
            if slot_i % 2:
                nsend[w, slot_i // 2] = g.astype(jnp.bfloat16)
                p_near[w][slot_i // 2] = copy(nsend.at[w, slot_i // 2], nrecv.at[w, slot_i // 2], sibling)
                p_near[w][slot_i // 2].start()
            else:
                pown[w, slot_i // 2] = g

    def prompt_far(w):
        p_far[w] = []
        for d in range(1, chips):
            p_near[w][d].wait_recv()
            psend[w, d - 1] = (pown[w, d] + nrecv[w, d].astype(jnp.float32)).astype(jnp.bfloat16)
            p_far[w].append(copy(psend.at[w, d - 1], precv.at[w, d - 1], chip_back[d]))
            p_far[w][-1].start()

    def octet_scatter(send, recv, place):
        out = []
        for e in range(1, GROUP):
            out.append(copy(send.at[place(lax.rem(local + e, GROUP))], recv.at[e - 1], octet[e]))
            out[-1].start()
        return out

    def octet_gather(copies, own, recv, stage, out, place):
        total = own[place(local)]
        for e in range(1, GROUP):
            copies[e - 1].wait_recv()
            total = total + recv[e - 1].astype(jnp.float32)
        stage[...] = total.astype(jnp.bfloat16)
        first = count[0]
        for e in range(1, GROUP):
            copy(stage, out.at[place(local)], octet[e]).start()
        out[place(local)] = total.astype(jnp.bfloat16)
        return first

    def octet_finish(first, out, place):
        for e in range(1, GROUP):
            ref = out.at[place(lax.rem(local + GROUP - e, GROUP))]
            pltpu.make_async_remote_copy(
                src_ref=ref, dst_ref=ref, send_sem=send_sem.at[first + e - 1], recv_sem=recv_sem.at[first + e - 1],
                device_id=octet[e], device_id_type=MESH,
            ).wait_recv()

    def relay_gather(copies, own, recv, stage, out):
        total = own[local]
        for e in range(1, GROUP):
            copies[e - 1].wait_recv()
            total = total + recv[e - 1].astype(jnp.float32)
        stage[...] = total.astype(jnp.bfloat16)
        first = count[0]
        for e in range(2, GROUP, 2):
            copy(stage, out.at[local], octet[e]).start()
        copy(stage, out.at[local], partner).start()
        out[local] = total.astype(jnp.bfloat16)
        return first

    def arrived(s, ref):
        pltpu.make_async_remote_copy(
            src_ref=ref, dst_ref=ref, send_sem=send_sem.at[s], recv_sem=recv_sem.at[s],
            device_id=partner, device_id_type=MESH,
        ).wait_recv()

    def relay_forward(first, out):
        passed = [first + QUAD - 1]
        for z in range(1, QUAD):
            piece = out.at[lax.rem(local + GROUP - 2 * z, GROUP)]
            arrived(first + z - 1, piece)
            passed.append(count[0])
            copy(piece, piece, partner).start()
        return passed

    def relay_finish(passed, out):
        for z in range(QUAD):
            arrived(passed[z], out.at[lax.rem(other + GROUP - 2 * z, GROUP)])

    def straight(member):
        return member

    def paired(member):
        return lax.rem(member, 2) * QUAD + member // 2

    eighth = length // GROUP

    def answer_terms(w, probs, right):
        for a in range(blocks):
            at = prompt + a * COLS
            g = jnp.dot(
                probs[at:at + COLS, a * COLS:], right[a * COLS:], preferred_element_type=jnp.float32
            ).reshape(COLS // eighth, eighth, hd)
            first = a * COLS // eighth
            aown[w, first:first + COLS // eighth] = g
            asend[w, first:first + COLS // eighth] = g.astype(jnp.bfloat16)
        return octet_scatter(asend.at[w], arecv.at[w], straight)

    av = answer_terms(1, pb, do_m)
    prompt_terms(1, pb, do_m)

    prompt_far(1)
    for c in [v_in[0]] + v_fwd:
        c.wait_recv()
    stores = []

    def keep(src, dst):
        stores.append(pltpu.make_async_copy(src, dst, load_sem.at[7 + len(stores)]))
        stores[-1].start()

    deltas = []
    for b in range(blocks):
        keys = prompt + (b + 1) * COLS
        mixed = contract(v_all[:keys], pb[:keys, cols(b)], 0, 0)
        lane = lax.broadcasted_iota(jnp.int32, mixed.shape, 1) + b * COLS
        mixed = jnp.where(lane < own_count, mixed, 0.0).astype(jnp.bfloat16).astype(jnp.float32)
        att_ref[cols(b)] = mixed.T.astype(jnp.bfloat16)
        dout_t = do_m[cols(b)].astype(jnp.float32).T
        deltas.append(jnp.sum(dout_t * mixed, axis=0, keepdims=True))

    keep(att_ref, att_out)
    def score_grads(b, at, size):
        dp = contract(v_all[at:at + size], do_m[cols(b)], 1, 1)
        ds = st[at:at + size, cols(b)] * (dp - deltas[b]) * factor
        dsb[at:at + size, cols(b)] = ds.astype(jnp.bfloat16)

    for b in range(blocks):
        for at, size in spans(b)[:n]:
            score_grads(b, at, size)
    prompt_terms(0, dsb, q_ref)
    for b in range(blocks):
        for at, size in spans(b)[n:]:
            score_grads(b, at, size)
    prompt_far(0)
    ak = answer_terms(0, dsb, q_ref)
    av_out = relay_gather(av, aown.at[1], arecv.at[1], ga_own.at[1], ga_ref.at[1])

    for b in range(blocks):
        keys = prompt + (b + 1) * COLS
        dq = contract(k_all[:keys], dsb[:keys, cols(b)], 0, 0)
        dq_ref[cols(b)] = dq.T.astype(jnp.bfloat16)
    keep(dq_ref, dq_out)

    for w in (1, 0):
        p_near[w][0].wait_recv()
        total = pown[w, 0] + nrecv[w, 0].astype(jnp.float32)
        for d in range(1, chips):
            p_far[w][d - 1].wait_recv()
            total = total + precv[w, d - 1].astype(jnp.float32)
        size = shard // QUAD
        for z in range(QUAD):
            pzown[w * QUAD + z] = total[z * size:(z + 1) * size]
            pzsend[w * QUAD + z] = total[z * size:(z + 1) * size].astype(jnp.bfloat16)

    ap = octet_scatter(pzsend, pzrecv, paired)
    av_out = relay_forward(av_out, ga_ref.at[1])
    ak_out = relay_gather(ak, aown.at[0], arecv.at[0], ga_own.at[0], ga_ref.at[0])
    ap_out = octet_gather(ap, pzown, pzrecv, gp_own, gp_ref, paired)
    ak_out = relay_forward(ak_out, ga_ref.at[0])
    relay_finish(av_out, ga_ref.at[1])
    keep(ga_ref.at[1], ga_out.at[1])
    relay_finish(ak_out, ga_ref.at[0])
    keep(ga_ref.at[0], ga_out.at[0])
    octet_finish(ap_out, gp_ref, paired)
    keep(gp_ref, gp_out)
    for c in stores:
        c.wait()
    for c in started:
        c.wait_send()


def fused(queries, answer_keys, answer_values, prompt_keys, prompt_values, out_grad, block_counts, n):
    length, hd = queries.shape
    shard = prompt_keys.shape[0]
    keys = n * shard + length
    eighth = length // GROUP
    piece = shard // QUAD
    bf, f32 = jnp.bfloat16, jnp.float32
    chips = n // 2
    sems = 2 * (2 * chips - 1) + 2 * (2 * chips - 1) + 6 * (GROUP - 1)
    hbm = pl.BlockSpec(memory_space=pl.ANY)
    return pl.pallas_call(
        functools.partial(kernel, n),
        out_shape=(
            jax.ShapeDtypeStruct((length, hd), bf),
            jax.ShapeDtypeStruct((length, hd), bf),
            jax.ShapeDtypeStruct((GROUP, piece, hd), bf),
            jax.ShapeDtypeStruct((2, GROUP, eighth, hd), bf),
        ),
        in_specs=[hbm] * 7,
        out_specs=(hbm,) * 4,
        scratch_shapes=[
            pltpu.VMEM((length, hd), bf),
            pltpu.VMEM((length, hd), bf),
            pltpu.VMEM((GROUP, piece, hd), bf),
            pltpu.VMEM((2, GROUP, eighth, hd), bf),
            pltpu.VMEM((piece, hd), bf),
            pltpu.VMEM((2, eighth, hd), bf),
            pltpu.VMEM((length, hd), bf),
            pltpu.VMEM((length, hd), bf),
            pltpu.SMEM(block_counts.shape, jnp.int32),
            pltpu.VMEM((keys, hd), bf),
            pltpu.VMEM((keys, hd), bf),
            pltpu.VMEM((length, hd), bf),
            pltpu.VMEM((keys, length), f32),
            pltpu.VMEM((keys, length), bf),
            pltpu.VMEM((keys, length), bf),
            pltpu.VMEM((2, chips, shard, hd), bf),
            pltpu.VMEM((2, chips, shard, hd), bf),
            pltpu.VMEM((2, chips, shard, hd), f32),
            pltpu.VMEM((2, chips - 1, shard, hd), bf),
            pltpu.VMEM((2, chips - 1, shard, hd), bf),
            pltpu.VMEM((2, GROUP, eighth, hd), f32),
            pltpu.VMEM((2, GROUP, eighth, hd), bf),
            pltpu.VMEM((2, GROUP - 1, eighth, hd), bf),
            pltpu.VMEM((GROUP, piece, hd), f32),
            pltpu.VMEM((GROUP, piece, hd), bf),
            pltpu.VMEM((GROUP - 1, piece, hd), bf),
            pltpu.SemaphoreType.DMA((sems,)),
            pltpu.SemaphoreType.DMA((sems,)),
            pltpu.SemaphoreType.DMA((12,)),
        ],
        compiler_params=pltpu.CompilerParams(
            collective_id=0, has_side_effects=True, vmem_limit_bytes=VMEM
        ),
    )(queries, answer_keys, answer_values, prompt_keys, prompt_values, out_grad, block_counts)


def store(att, dq, gp, ga, *refs):
    outs, held, load, save = refs[:6], refs[6:12], refs[12], refs[13]
    sources = (ga.at[0], ga.at[1], att, dq, gp.at[0], gp.at[1])
    copies = [
        (pltpu.make_async_copy(src, mid, load.at[s]), pltpu.make_async_copy(mid, dst, save.at[s]))
        for s, (src, mid, dst) in enumerate(zip(sources, held, outs))
    ]
    for c, _ in copies:
        c.start()
    for c, then in copies:
        c.wait()
        then.start()
    for _, c in copies:
        c.wait()


def write_out(att, dq, gp, ga):
    shapes = [jax.ShapeDtypeStruct(x.shape, x.dtype) for x in (ga[0], ga[1], att, dq, gp[0], gp[1])]
    results = pl.pallas_call(
        store,
        out_shape=shapes,
        in_specs=[pl.BlockSpec(memory_space=pl.ANY)] * 4,
        out_specs=[pl.BlockSpec(memory_space=pl.ANY)] * 6,
        scratch_shapes=[pltpu.VMEM(x.shape, x.dtype) for x in shapes]
        + [pltpu.SemaphoreType.DMA((6,)), pltpu.SemaphoreType.DMA((6,))],
        compiler_params=pltpu.CompilerParams(vmem_limit_bytes=VMEM),
    )(att, dq, gp, ga)
    return results[2], results[3], results[4:], results[:2]


def shards(n, groups, queries, answer_keys, answer_values, prompt_keys, prompt_values, out_grad, block_counts):
    hd = queries.shape[2]
    length = queries.shape[1]
    shard = prompt_keys.shape[0]
    kv = [answer_keys[0], answer_values[0], prompt_keys, prompt_values]
    if groups > 1:
        kv_group = lax.axis_index("tp") // GROUP
        kv = [lax.dynamic_slice_in_dim(x, kv_group * hd, hd, 1) for x in kv]
    attended, query_grad, gp, ga = fused(queries[0], *kv, out_grad[0], block_counts, n)
    gp = gp.reshape(2, shard, hd)
    attended, query_grad, gp, ga = write_out(attended, query_grad, gp, ga)
    outs = [gp[0].reshape(shard, hd), gp[1].reshape(shard, hd), ga[0].reshape(length, hd), ga[1].reshape(length, hd)]
    if groups > 1:
        sets = [[g * GROUP + i for g in range(groups)] for i in range(GROUP)]
        outs = [lax.all_gather(x, "tp", axis=1, tiled=True, axis_index_groups=sets) for x in outs]
    return attended[None], query_grad[None], outs[0], outs[1], outs[2][None], outs[3][None]


def solution(mesh):
    n, tp = mesh.shape["comp"], mesh.shape["tp"]
    return jax.shard_map(
        functools.partial(shards, n, tp // GROUP),
        mesh=mesh,
        in_specs=(
            P("comp", None, "tp"),
            P("comp", None, None),
            P("comp", None, None),
            P("comp", None),
            P("comp", None),
            P("comp", None, "tp"),
            P(),
        ),
        out_specs=(
            P("comp", None, "tp"),
            P("comp", None, "tp"),
            P("comp", None),
            P("comp", None),
            P("comp", None, None),
            P("comp", None, None),
        ),
        check_vma=False,
    )
```
